32 devices in a mesh: mob: 2 (over x), imm: 16 (over z, y, core).
Axes of the slice: x: 2, y: 2, z: 4, core: 2. Of those that a mesh axis runs over, the one named last changes fastest.
Arguments:
- mobile_positions: float32 [512, 3, 128], P(('mob', 'imm')), may hold values from 0 to 4
- walk: float32 [2, 512, 3, 128], P(None, ('mob', 'imm')), may hold values from -1.8 to 1.8
- mobile_conc: float32 [512, 8, 128], P(('mob', 'imm')), may hold values from 0 to 2
- matrix_positions: float32 [512, 3, 128], P(('mob', 'imm')), may hold values from 0 to 4
- matrix_conc: float32 [512, 8, 128], P(('mob', 'imm')), may hold values from 0 to 2
- pair_rows: int32 [2, 16, 512], P('mob', 'imm'), may hold values from 0 to 255, as said below
- pair_cols: int32 [2, 16, 512], P('mob', 'imm'), may hold values from 0 to 31
- pair_counts: int32 [2, 16], P('mob', 'imm'), may hold values from 128 to 512, as said below
Outputs:
- mobile_after: float32 [512, 8, 128], P(('mob', 'imm'))
- matrix_after: float32 [512, 8, 128], P(('mob', 'imm'))
The draws below stay inside these ranges and needn't reach their ends.
Inputs may be any that keep to these rules, and one draw needn't show every extreme that they name: Within one device the listed pairs (pair_rows, pair_cols) are distinct. `pair_counts`: in every draw some device uses all 512 slots.
All inputs are finite; a program needn't handle non-finite values.
Results may differ from the reference program's by a relative error of at most 0.0003.
Values sent between devices are 32-bit elements; how exact they have to be, the bound alone decides.
A program may use at most 64 MiB of HBM per device.

```python
import math
import jax
import jax.numpy as jnp
from jax import lax

PART = 128
SOLUTES = 8
MC_DEV = 16
IC_DEV = 16
PAIRS_DEV = 512
MCELLS = 512
ICELLS = 512
N_MOB = 2
N_IMM = 16


def pair_table(key):
    key = jax.random.fold_in(key, 11)
    tiles = N_MOB * N_IMM
    group_m = MC_DEV * N_IMM
    group_i = IC_DEV * N_MOB
    keys = jax.random.split(key, tiles)

    def one_tile(tile_key):
        key_a, key_b = jax.random.split(tile_key)
        order = jax.random.permutation(key_a, jnp.arange(group_m, dtype=jnp.int32))
        offset = jax.random.randint(key_b, (group_m,), 0, group_i, dtype=jnp.int32)
        slot = jnp.arange(PAIRS_DEV, dtype=jnp.int32)
        rows = order[slot % group_m]
        cols = (offset[slot % group_m] + slot // group_m) % group_i
        return (rows, cols)
    rows, cols = jax.vmap(one_tile)(keys)
    return (rows.reshape(N_MOB, N_IMM, PAIRS_DEV), cols.reshape(N_MOB, N_IMM, PAIRS_DEV))


def draw_pair_rows(key, part):
    return pair_table(key)[0]


def draw_pair_cols(key, part):
    return pair_table(key)[1]


def draw_pair_counts(key, part):
    key = jax.random.fold_in(key, 23)
    key_a, key_b, key_c = jax.random.split(key, 3)
    tiles = N_MOB * N_IMM
    base = PAIRS_DEV // 4 + jax.random.randint(key_a, (tiles,), 0, PAIRS_DEV // 4 + 1, dtype=jnp.int32)
    full = jax.random.randint(key_b, (tiles,), 0, 8, dtype=jnp.int32) == 0
    chosen = jax.random.randint(key_c, (), 0, tiles, dtype=jnp.int32)
    full = full | (jnp.arange(tiles, dtype=jnp.int32) == chosen)
    counts = jnp.where(full, PAIRS_DEV, base).astype(jnp.int32)
    return counts.reshape(N_MOB, N_IMM)


def shard_levels(rng, extent, cuts, low, top_value):
    def one(axis_at, parts):
        draws = jax.random.uniform(jax.random.fold_in(jax.random.fold_in(rng, 6), axis_at), (parts,), jnp.float32, low / len(cuts), top_value / len(cuts))
        return jnp.repeat(jnp.exp(draws), extent[axis_at] // parts).reshape((-1,) + (1,) * (len(extent) - axis_at - 1))

    gain = one(*cuts[0])
    for cut in cuts[1:]:
        gain = gain * one(*cut)
    return gain


def centred(stream_key, shape, deviation, bound, cuts=(), kind=jnp.bfloat16):
    result = deviation * jax.random.normal(stream_key, shape, jnp.float32)
    if cuts:
        result = result * shard_levels(stream_key, shape, cuts, -0.22, 0.18)
    return jnp.clip(result, -bound, bound).astype(kind)


def setup_inputs(seed: int = 0) -> dict:
    seeds = jax.random.split(jax.random.key(seed), 9)
    return {
        "mobile_positions": jnp.clip(4.0 * jax.random.uniform(seeds[0], (MCELLS, 3, PART), jnp.float32) ** shard_levels(seeds[0], (MCELLS, 3, PART), ((0, 32),), -0.2, 0.2), 0.0, 4.0),
        "walk": centred(seeds[1], (2, MCELLS, 3, PART), 0.3, 1.8, ((1, 32),), jnp.float32),
        "mobile_conc": jnp.clip(2.0 * jax.random.uniform(seeds[2], (MCELLS, SOLUTES, PART), jnp.float32) ** shard_levels(seeds[2], (MCELLS, SOLUTES, PART), ((0, 32),), -0.2, 0.2), 0.0, 2.0),
        "matrix_positions": jnp.clip(4.0 * jax.random.uniform(seeds[3], (ICELLS, 3, PART), jnp.float32) ** shard_levels(seeds[3], (ICELLS, 3, PART), ((0, 32),), -0.2, 0.2), 0.0, 4.0),
        "matrix_conc": jnp.clip(2.0 * jax.random.uniform(seeds[4], (ICELLS, SOLUTES, PART), jnp.float32) ** shard_levels(seeds[4], (ICELLS, SOLUTES, PART), ((0, 32),), -0.2, 0.2), 0.0, 2.0),
        "pair_rows": draw_pair_rows(jax.random.fold_in(seeds[8], 71), 0),
        "pair_cols": draw_pair_cols(jax.random.fold_in(seeds[8], 71), 0),
        "pair_counts": draw_pair_counts(jax.random.fold_in(seeds[8], 71), 0),
    }


RATE = 1.0 / 512.0


def pair_gains(mob_pos, imm_pos, mob_conc, imm_conc, valid):
    diff_x = mob_pos[:, 0, :, None] - imm_pos[:, 0, None, :]
    diff_y = mob_pos[:, 1, :, None] - imm_pos[:, 1, None, :]
    diff_z = mob_pos[:, 2, :, None] - imm_pos[:, 2, None, :]
    weight = jnp.exp(-0.5 * (diff_x * diff_x + diff_y * diff_y + diff_z * diff_z)) * valid[:, None, None]
    toward_m = jnp.einsum("kab,ksb->ksa", weight, imm_conc, precision=lax.Precision.HIGHEST)
    toward_i = jnp.einsum("kab,ksa->ksb", weight, mob_conc, precision=lax.Precision.HIGHEST)
    gain_m = RATE * (toward_m - jnp.sum(weight, axis=2)[:, None, :] * mob_conc)
    gain_i = RATE * (toward_i - jnp.sum(weight, axis=1)[:, None, :] * imm_conc)
    return gain_m, gain_i


def one_step(positions, mob_conc, imm_pos, imm_conc, mob_cells, imm_cells, valid):
    def scan_fn(carry, blk):
        delta_m, delta_i = carry
        mcell, icell, used = blk
        gain_m, gain_i = pair_gains(positions[mcell], imm_pos[icell], mob_conc[mcell], imm_conc[icell], used)
        return (delta_m.at[mcell].add(gain_m), delta_i.at[icell].add(gain_i)), None

    start = (jnp.zeros_like(mob_conc), jnp.zeros_like(imm_conc))
    (delta_m, delta_i), _ = lax.scan(scan_fn, start, (mob_cells, imm_cells, valid))
    return mob_conc + delta_m, imm_conc + delta_i


def reference(mobile_positions, walk, mobile_conc, matrix_positions, matrix_conc, pair_rows, pair_cols, pair_counts):
    moved_one = mobile_positions + walk[0]
    moved_two = moved_one + walk[1]
    tile_m = jnp.arange(N_MOB).astype(jnp.int32)[:, None, None]
    tile_i = jnp.arange(N_IMM).astype(jnp.int32)[None, :, None]
    mob_cells = tile_m * (N_IMM * MC_DEV) + pair_rows
    imm_cells = ((pair_cols // IC_DEV) * N_IMM + tile_i) * IC_DEV + pair_cols % IC_DEV
    slots = jnp.arange(PAIRS_DEV).astype(jnp.int32)[None, None, :]
    valid = jnp.where(slots < pair_counts[:, :, None], 1.0, 0.0).astype(jnp.float32)
    total = N_MOB * N_IMM * PAIRS_DEV
    blk = math.gcd(total, 512)
    mob_cells = mob_cells.reshape(-1, blk).astype(jnp.int32)
    imm_cells = imm_cells.reshape(-1, blk).astype(jnp.int32)
    valid = valid.reshape(-1, blk)
    mob_c, imm_c = one_step(moved_one, mobile_conc, matrix_positions, matrix_conc, mob_cells, imm_cells, valid)
    mob_c, imm_c = one_step(moved_two, mob_c, matrix_positions, imm_c, mob_cells, imm_cells, valid)
    return mob_c, imm_c
```

```python
import functools
import math

import jax
import jax.numpy as jnp
from jax import lax
from jax.experimental import pallas as pl
from jax.experimental.pallas import tpu as pltpu
from jax.sharding import PartitionSpec as P

RATE = 1.0 / 512.0
SCALE = math.sqrt(0.5 * math.log2(math.e))
CENTRE = 2.0
MESH = pl.DeviceIdType.MESH
VMEM_LIMIT = 48 * 1024 * 1024
UNROLL = 4
GROUPS = 6


class Place:
    def __init__(self, n_mob, n_imm):
        rest = n_imm // 2
        nb = 1
        while nb * nb * 4 <= rest:
            nb *= 2
        self.nm, self.nb, self.na = n_mob, nb, rest // nb
        self.p = lax.axis_index("mob")
        q = lax.axis_index("imm")
        self.core = lax.rem(q, 2)
        chip = lax.div(q, 2)
        self.b = lax.rem(chip, nb)
        self.a = lax.div(chip, nb)

    def am(self, d):
        return lax.rem(self.a + (d + self.na), self.na)

    def bm(self, d):
        return lax.rem(self.b + (d + self.nb), self.nb)

    def pm(self, d):
        return lax.rem(self.p + (d + self.nm), self.nm)

    def dev(self, a, b, core):
        return (self.p, (a * self.nb + b) * 2 + core)

    def sibling(self):
        return self.dev(self.a, self.b, 1 - self.core)

    def across(self, d):
        return (self.pm(d), (self.a * self.nb + self.b) * 2 + self.core)

    def barrier(self):
        sem = pltpu.get_barrier_semaphore()
        peers = [self.sibling()]
        peers += [self.dev(self.a, self.bm(d), self.core) for d in range(1, self.nb)]
        peers += [self.dev(self.am(d), self.b, self.core) for d in range(1, self.na)]
        peers += [self.across(d) for d in range(1, self.nm)]
        for peer in peers:
            pl.semaphore_signal(sem, inc=1, device_id=peer, device_id_type=MESH)
        pl.semaphore_wait(sem, len(peers))


def remote(src, dst, send, recv, device):
    copy = pltpu.make_async_remote_copy(
        src_ref=src, dst_ref=dst, send_sem=send, recv_sem=recv, device_id=device, device_id_type=MESH
    )
    copy.start()
    return copy


def gather_imm(at, refs, sems):
    a_send, a_recv, b_send, b_recv, c_send, c_recv = sems
    na, nb = at.na, at.nb
    sends, a_copies, b_copies, c_copies = [], {}, {}, {}
    for da in range(1, na):
        for i, g in enumerate(refs):
            block = g.at[at.a, at.b, at.core]
            a_copies[da, i] = remote(
                block, block, a_send.at[i, da], a_recv.at[i, da], at.dev(at.am(da), at.b, at.core)
            )
    for da in range(na):
        for i, g in enumerate(refs):
            if da:
                a_copies[da, i].wait_recv()
            block = g.at[at.am(-da), at.b, at.core]
            for db in range(1, nb):
                b_copies[da, db, i] = remote(
                    block, block, b_send.at[i, da, db], b_recv.at[i, da, db], at.dev(at.a, at.bm(db), at.core)
                )
            c_copies[da, 0, i] = remote(
                block, block, c_send.at[i, da, 0], c_recv.at[i, da, 0], at.sibling()
            )
    for da in range(na):
        for db in range(1, nb):
            for i, g in enumerate(refs):
                b_copies[da, db, i].wait_recv()
                block = g.at[at.am(-da), at.bm(-db), at.core]
                c_copies[da, db, i] = remote(
                    block, block, c_send.at[i, da, db], c_recv.at[i, da, db], at.sibling()
                )
    for copy in c_copies.values():
        copy.wait_recv()
    for copies in (a_copies, b_copies, c_copies):
        for copy in copies.values():
            copy.wait_send()


def gather_mob_start(at, refs, send, recv):
    copies = []
    for dp in range(1, at.nm):
        for i, g in enumerate(refs):
            block = g.at[at.p]
            copies.append(remote(block, block, send.at[i, dp], recv.at[i, dp], at.across(dp)))
    return copies


def reduce_mob_start(at, part, land, send, recv):
    return [
        remote(part.at[at.pm(dp)], land.at[dp], send.at[dp], recv.at[dp], at.across(dp))
        for dp in range(1, at.nm)
    ]


def reduce_imm(at, part, land_c, land_b, land_a, out_b, out_a, sems):
    a_send, a_recv, b_send, b_recv, c_send, c_recv = sems
    na, nb = at.na, at.nb
    order = list(range(1, na)) + [0]
    a_copies, b_copies, c_copies = {}, {}, {}
    for db in list(range(1, nb)) + [0]:
        for da in order:
            c_copies[da, db] = remote(
                part.at[at.am(da), at.bm(db), 1 - at.core],
                land_c.at[da, db],
                c_send.at[da, db],
                c_recv.at[da, db],
                at.sibling(),
            )
    for da in order:
        for db in range(1, nb):
            c_copies[da, db].wait_recv()
            out_b[da, db] = part[at.am(da), at.bm(db), at.core] + land_c[da, db]
            b_copies[da, db] = remote(
                out_b.at[da, db],
                land_b.at[da, db],
                b_send.at[da, db],
                b_recv.at[da, db],
                at.dev(at.a, at.bm(db), at.core),
            )
    total = None
    for da in order:
        c_copies[da, 0].wait_recv()
        here = part[at.am(da), at.b, at.core] + land_c[da, 0]
        for db in range(1, nb):
            b_copies[da, db].wait_recv()
            here = here + land_b[da, db]
        if da:
            out_a[da] = here
            a_copies[da] = remote(
                out_a.at[da], land_a.at[da], a_send.at[da], a_recv.at[da], at.dev(at.am(da), at.b, at.core)
            )
        else:
            total = here
    for da in range(1, na):
        a_copies[da].wait_recv()
        total = total + land_a[da]
    for copies in (a_copies, b_copies, c_copies):
        for copy in copies.values():
            copy.wait_send()
    return total


def first_gather(n_mob, n_imm, mpos, walk, mconc, ipos, iconc, g_pos, g_conc, h_pos, h_conc, *sems):
    at = Place(n_mob, n_imm)
    own = g_pos.at[at.a, at.b, at.core]
    moved = mpos[...]
    for step in range(2):
        moved = moved + walk[step]
        x = (moved - CENTRE) * SCALE
        own[:, 4 * step : 4 * step + 3, :] = x
        own[:, 4 * step + 3 : 4 * step + 4, :] = -jnp.sum(x * x, axis=1, keepdims=True)
    g_conc[at.a, at.b, at.core] = mconc[...]
    h_own = h_pos.at[at.p]
    y = (ipos[...] - CENTRE) * SCALE
    h_own[:, 0:3, :] = 2.0 * y
    h_own[:, 3:4, :] = jnp.ones_like(y[:, 0:1, :])
    h_own[:, 4:5, :] = -jnp.sum(y * y, axis=1, keepdims=True)
    h_own[:, 5:8, :] = jnp.zeros_like(y)
    h_conc[at.p] = iconc[...]
    at.barrier()
    mob = gather_mob_start(at, (h_pos, h_conc), *sems[6:])
    gather_imm(at, (g_conc, g_pos), sems[:6])
    for copy in mob:
        copy.wait()


def exchange(n_mob, n_imm, part_m, part_i, conc_m, conc_i, own_m, own_i, g_conc, h_conc,
             land_c, land_b, land_a, out_b, out_a, land_m, *sems):
    at = Place(n_mob, n_imm)
    at.barrier()
    mob = reduce_mob_start(at, part_i, land_m, *sems[6:8])
    total = conc_m[...] + reduce_imm(at, part_m, land_c, land_b, land_a, out_b, out_a, sems[:6])
    own_m[...] = total
    g_conc[at.a, at.b, at.core] = total
    total = conc_i[...] + part_i[at.p]
    for dp, copy in enumerate(mob, 1):
        copy.wait()
        total = total + land_m[dp]
    own_i[...] = total
    h_conc[at.p] = total
    mob = gather_mob_start(at, (h_conc,), *sems[8:10])
    gather_imm(at, (g_conc,), sems[10:16])
    for copy in mob:
        copy.wait()


def last_reduce(n_mob, n_imm, part_m, part_i, conc_m, conc_i, own_m, own_i,
                land_c, land_b, land_a, out_b, out_a, land_m, *sems):
    at = Place(n_mob, n_imm)
    at.barrier()
    mob = reduce_mob_start(at, part_i, land_m, *sems[6:8])
    own_m[...] = conc_m[...] + reduce_imm(at, part_m, land_c, land_b, land_a, out_b, out_a, sems[:6])
    total = conc_i[...] + part_i[at.p]
    for dp, copy in enumerate(mob, 1):
        copy.wait()
        total = total + land_m[dp]
    own_i[...] = total


def split3(x):
    high = x.astype(jnp.bfloat16).astype(jnp.float32)
    rest = x - high
    mid = rest.astype(jnp.bfloat16).astype(jnp.float32)
    return high, mid, rest - mid


def conc_rows(conc):
    high = conc.astype(jnp.bfloat16).astype(jnp.float32)
    ones = jnp.ones_like(conc)
    return jnp.concatenate([high, conc - high, ones, ones], axis=0).astype(jnp.bfloat16)


def pair_loop(step, rows, cols, count, x_pos, x_conc, y_pos, y_conc, gain_m, gain_i, y_split):
    gain_m[...] = jnp.zeros_like(gain_m)
    gain_i[...] = jnp.zeros_like(gain_i)

    def prepare(c, carry):
        h, m, l = split3(y_pos[c])
        zeros = jnp.zeros((128 - 8 * GROUPS, 128), jnp.float32)
        stacked = jnp.concatenate([h, h, h, m, m, l, zeros], axis=0)
        y_split[c] = stacked.T.astype(jnp.bfloat16)
        return carry

    lax.fori_loop(0, y_pos.shape[0], prepare, 0)
    row = lax.broadcasted_iota(jnp.int32, (8, 128), 0)
    keep = row < 4
    unit = jnp.where(row == 4, 1.0, 0.0).astype(jnp.float32)
    zeros = jnp.zeros((128 - 8 * GROUPS, 128), jnp.float32)
    used = count[0, 0]

    def body(block, carry):
        results = []
        for u in range(UNROLL):
            k = block * UNROLL + u
            r, c = rows[0, 0, k], cols[0, 0, k]
            x = x_pos[r]
            if step:
                x = pltpu.roll(x, 4, 0)
            h, m, l = split3(jnp.where(keep, x, unit))
            x_split = jnp.concatenate([h, m, l, h, m, h, zeros], axis=0).astype(jnp.bfloat16)
            power = jnp.dot(y_split[c], x_split, preferred_element_type=jnp.float32)
            weight = jnp.exp2(power).astype(jnp.bfloat16)
            cm, ci = x_conc[r], y_conc[c]
            to_m = jnp.dot(conc_rows(ci), weight, preferred_element_type=jnp.float32)
            to_i = lax.dot_general(
                conc_rows(cm), weight, (((1,), (1,)), ((), ())), preferred_element_type=jnp.float32
            )
            rate = jnp.where(k < used, RATE, 0.0).astype(jnp.float32)
            add_m = rate * (to_m[0:8] + to_m[8:16] - to_m[16:24] * cm)
            add_i = rate * (to_i[0:8] + to_i[8:16] - to_i[16:24] * ci)
            results.append((r, c, add_m, add_i))
        for r, c, add_m, add_i in results:
            gain_m[r] += add_m
            gain_i[c] += add_i
        return carry

    lax.fori_loop(0, lax.div(used + (UNROLL - 1), UNROLL), body, 0)


def on_device(n_mob, n_imm, mpos, walk, mconc, ipos, iconc, rows, cols, counts):
    rest = n_imm // 2
    nb = 1
    while nb * nb * 4 <= rest:
        nb *= 2
    na = rest // nb
    f32 = jnp.float32
    mc, solutes, part = mconc.shape
    ic = iconc.shape[0]
    vmem = pl.BlockSpec(memory_space=pltpu.VMEM)
    smem = pl.BlockSpec(memory_space=pltpu.SMEM)
    dma = pltpu.SemaphoreType.DMA

    def params(ident):
        return pltpu.CompilerParams(collective_id=ident, has_side_effects=True, vmem_limit_bytes=VMEM_LIMIT)

    def gather_sems(refs):
        return [dma((refs, na))] * 2 + [dma((refs, na, nb))] * 4

    reduce_sems = [dma((na,))] * 2 + [dma((na, nb))] * 4
    cell_m = (mc, solutes, part)
    cell_i = (ic, solutes, part)
    all_m = jax.ShapeDtypeStruct((na, nb, 2) + cell_m, f32)
    all_i = jax.ShapeDtypeStruct((n_mob,) + cell_i, f32)
    g_pos, g_conc, h_pos, h_conc = pl.pallas_call(
        functools.partial(first_gather, n_mob, n_imm),
        out_shape=(all_m, all_m, all_i, all_i),
        in_specs=[vmem] * 5,
        out_specs=(vmem,) * 4,
        scratch_shapes=gather_sems(2) + [dma((2, n_mob))] * 2,
        compiler_params=params(0),
    )(mpos, walk, mconc, ipos, iconc)

    flat_m = (n_imm * mc, solutes, part)
    flat_i = (n_mob * ic, solutes, part)

    def pairs(step, x_conc, y_conc):
        gains = pl.pallas_call(
            functools.partial(pair_loop, step),
            out_shape=(jax.ShapeDtypeStruct(flat_m, f32), jax.ShapeDtypeStruct(flat_i, f32)),
            in_specs=[smem] * 3 + [vmem] * 4,
            out_specs=(vmem,) * 2,
            scratch_shapes=[pltpu.VMEM((flat_i[0], part, 128), jnp.bfloat16)],
            compiler_params=pltpu.CompilerParams(vmem_limit_bytes=VMEM_LIMIT),
        )(
            rows,
            cols,
            counts,
            g_pos.reshape(flat_m),
            x_conc.reshape(flat_m),
            h_pos.reshape(flat_i),
            y_conc.reshape(flat_i),
        )
        return gains[0].reshape(all_m.shape), gains[1].reshape(all_i.shape)

    lands = [
        pltpu.VMEM((na, nb) + cell_m, f32),
        pltpu.VMEM((na, nb) + cell_m, f32),
        pltpu.VMEM((na,) + cell_m, f32),
        pltpu.VMEM((na, nb) + cell_m, f32),
        pltpu.VMEM((na,) + cell_m, f32),
        pltpu.VMEM((n_mob,) + cell_i, f32),
    ]
    own = (jax.ShapeDtypeStruct(cell_m, f32), jax.ShapeDtypeStruct(cell_i, f32))
    part_m, part_i = pairs(0, g_conc, h_conc)
    own_m, own_i, g_conc, h_conc = pl.pallas_call(
        functools.partial(exchange, n_mob, n_imm),
        out_shape=own + (all_m, all_i),
        in_specs=[vmem] * 4,
        out_specs=(vmem,) * 4,
        scratch_shapes=lands + reduce_sems + [dma((n_mob,))] * 2 + [dma((1, n_mob))] * 2 + gather_sems(1),
        compiler_params=params(1),
    )(part_m, part_i, mconc, iconc)
    part_m, part_i = pairs(1, g_conc, h_conc)
    return pl.pallas_call(
        functools.partial(last_reduce, n_mob, n_imm),
        out_shape=own,
        in_specs=[vmem] * 4,
        out_specs=(vmem,) * 2,
        scratch_shapes=lands + reduce_sems + [dma((n_mob,))] * 2,
        compiler_params=params(2),
    )(part_m, part_i, own_m, own_i)


def solution(mesh):
    return jax.shard_map(
        functools.partial(on_device, mesh.shape["mob"], mesh.shape["imm"]),
        mesh=mesh,
        in_specs=(
            P(("mob", "imm"), None, None),
            P(None, ("mob", "imm"), None, None),
            P(("mob", "imm"), None, None),
            P(("mob", "imm"), None, None),
            P(("mob", "imm"), None, None),
            P("mob", "imm", None),
            P("mob", "imm", None),
            P("mob", "imm"),
        ),
        out_specs=(P(("mob", "imm"), None, None), P(("mob", "imm"), None, None)),
        check_vma=False,
    )
```

```python
import functools
import math

import jax
import jax.numpy as jnp
from jax import lax
from jax.experimental import pallas as pl
from jax.experimental.pallas import tpu as pltpu
from jax.sharding import PartitionSpec as P

RATE = 1.0 / 512.0
SCALE = math.sqrt(0.5 * math.log2(math.e))
CENTRE = 2.0
MESH = pl.DeviceIdType.MESH
VMEM_LIMIT = 48 * 1024 * 1024
UNROLL = 16
GROUPS = 6


class Place:
    def __init__(self, n_mob, n_imm):
        rest = n_imm // 2
        nb = 1
        while nb * nb * 4 <= rest:
            nb *= 2
        self.nm, self.nb, self.na = n_mob, nb, rest // nb
        self.p = lax.axis_index("mob")
        q = lax.axis_index("imm")
        self.core = lax.rem(q, 2)
        chip = lax.div(q, 2)
        self.b = lax.rem(chip, nb)
        self.a = lax.div(chip, nb)

    def am(self, d):
        return lax.rem(self.a + (d + self.na), self.na)

    def bm(self, d):
        return lax.rem(self.b + (d + self.nb), self.nb)

    def pm(self, d):
        return lax.rem(self.p + (d + self.nm), self.nm)

    def dev(self, a, b, core):
        return (self.p, (a * self.nb + b) * 2 + core)

    def sibling(self):
        return self.dev(self.a, self.b, 1 - self.core)

    def across(self, d):
        return (self.pm(d), (self.a * self.nb + self.b) * 2 + self.core)

    def barrier(self):
        sem = pltpu.get_barrier_semaphore()
        peers = [self.sibling()]
        peers += [self.dev(self.a, self.bm(d), self.core) for d in range(1, self.nb)]
        peers += [self.dev(self.am(d), self.b, self.core) for d in range(1, self.na)]
        peers += [self.across(d) for d in range(1, self.nm)]
        for peer in peers:
            pl.semaphore_signal(sem, inc=1, device_id=peer, device_id_type=MESH)
        pl.semaphore_wait(sem, len(peers))


def remote(src, dst, send, recv, device):
    copy = pltpu.make_async_remote_copy(
        src_ref=src, dst_ref=dst, send_sem=send, recv_sem=recv, device_id=device, device_id_type=MESH
    )
    copy.start()
    return copy


def gather_imm(at, refs, sems):
    a_send, a_recv, b_send, b_recv, c_send, c_recv = sems
    na, nb = at.na, at.nb
    sends, a_copies, b_copies, c_copies = [], {}, {}, {}
    for da in range(1, na):
        for i, g in enumerate(refs):
            block = g.at[at.a, at.b, at.core]
            a_copies[da, i] = remote(
                block, block, a_send.at[i, da], a_recv.at[i, da], at.dev(at.am(da), at.b, at.core)
            )
    for da in range(na):
        for i, g in enumerate(refs):
            if da:
                a_copies[da, i].wait_recv()
            block = g.at[at.am(-da), at.b, at.core]
            for db in range(1, nb):
                b_copies[da, db, i] = remote(
                    block, block, b_send.at[i, da, db], b_recv.at[i, da, db], at.dev(at.a, at.bm(db), at.core)
                )
            c_copies[da, 0, i] = remote(
                block, block, c_send.at[i, da, 0], c_recv.at[i, da, 0], at.sibling()
            )
    for da in range(na):
        for db in range(1, nb):
            for i, g in enumerate(refs):
                b_copies[da, db, i].wait_recv()
                block = g.at[at.am(-da), at.bm(-db), at.core]
                c_copies[da, db, i] = remote(
                    block, block, c_send.at[i, da, db], c_recv.at[i, da, db], at.sibling()
                )
    for copy in c_copies.values():
        copy.wait_recv()
    for copies in (a_copies, b_copies, c_copies):
        for copy in copies.values():
            copy.wait_send()


def gather_mob_start(at, refs, send, recv):
    copies = []
    for dp in range(1, at.nm):
        for i, g in enumerate(refs):
            block = g.at[at.p]
            copies.append(remote(block, block, send.at[i, dp], recv.at[i, dp], at.across(dp)))
    return copies


def reduce_mob_start(at, part, land, send, recv):
    return [
        remote(part.at[at.pm(dp)], land.at[dp], send.at[dp], recv.at[dp], at.across(dp))
        for dp in range(1, at.nm)
    ]


def reduce_imm(at, part, land_c, land_b, land_a, out_b, out_a, sems):
    a_send, a_recv, b_send, b_recv, c_send, c_recv = sems
    na, nb = at.na, at.nb
    order = list(range(1, na)) + [0]
    a_copies, b_copies, c_copies = {}, {}, {}
    for db in list(range(1, nb)) + [0]:
        for da in order:
            c_copies[da, db] = remote(
                part.at[at.am(da), at.bm(db), 1 - at.core],
                land_c.at[da, db],
                c_send.at[da, db],
                c_recv.at[da, db],
                at.sibling(),
            )
    for da in order:
        for db in range(1, nb):
            c_copies[da, db].wait_recv()
            out_b[da, db] = part[at.am(da), at.bm(db), at.core] + land_c[da, db]
            b_copies[da, db] = remote(
                out_b.at[da, db],
                land_b.at[da, db],
                b_send.at[da, db],
                b_recv.at[da, db],
                at.dev(at.a, at.bm(db), at.core),
            )
    total = None
    for da in order:
        c_copies[da, 0].wait_recv()
        here = part[at.am(da), at.b, at.core] + land_c[da, 0]
        for db in range(1, nb):
            b_copies[da, db].wait_recv()
            here = here + land_b[da, db]
        if da:
            out_a[da] = here
            a_copies[da] = remote(
                out_a.at[da], land_a.at[da], a_send.at[da], a_recv.at[da], at.dev(at.am(da), at.b, at.core)
            )
        else:
            total = here
    for da in range(1, na):
        a_copies[da].wait_recv()
        total = total + land_a[da]
    for copies in (a_copies, b_copies, c_copies):
        for copy in copies.values():
            copy.wait_send()
    return total


def first_gather(n_mob, n_imm, mpos, walk, mconc, ipos, iconc, g_pos, g_conc, h_pos, h_conc, *sems):
    at = Place(n_mob, n_imm)
    own = g_pos.at[at.a, at.b, at.core]
    moved = mpos[...]
    for step in range(2):
        moved = moved + walk[step]
        x = (moved - CENTRE) * SCALE
        own[:, 4 * step : 4 * step + 3, :] = x
        own[:, 4 * step + 3 : 4 * step + 4, :] = -jnp.sum(x * x, axis=1, keepdims=True)
    g_conc[at.a, at.b, at.core] = mconc[...]
    h_own = h_pos.at[at.p]
    y = (ipos[...] - CENTRE) * SCALE
    h_own[:, 0:3, :] = 2.0 * y
    h_own[:, 3:4, :] = jnp.ones_like(y[:, 0:1, :])
    h_own[:, 4:5, :] = -jnp.sum(y * y, axis=1, keepdims=True)
    h_own[:, 5:8, :] = jnp.zeros_like(y)
    h_conc[at.p] = iconc[...]
    at.barrier()
    mob = gather_mob_start(at, (h_pos, h_conc), *sems[6:])
    gather_imm(at, (g_conc, g_pos), sems[:6])
    for copy in mob:
        copy.wait()


def exchange(n_mob, n_imm, part_m, part_i, conc_m, conc_i, own_m, own_i, g_conc, h_conc,
             land_c, land_b, land_a, out_b, out_a, land_m, *sems):
    at = Place(n_mob, n_imm)
    at.barrier()
    mob = reduce_mob_start(at, part_i, land_m, *sems[6:8])
    total = conc_m[...] + reduce_imm(at, part_m, land_c, land_b, land_a, out_b, out_a, sems[:6])
    own_m[...] = total
    g_conc[at.a, at.b, at.core] = total
    total = conc_i[...] + part_i[at.p]
    for dp, copy in enumerate(mob, 1):
        copy.wait()
        total = total + land_m[dp]
    own_i[...] = total
    h_conc[at.p] = total
    mob = gather_mob_start(at, (h_conc,), *sems[8:10])
    gather_imm(at, (g_conc,), sems[10:16])
    for copy in mob:
        copy.wait()


def last_reduce(n_mob, n_imm, part_m, part_i, conc_m, conc_i, own_m, own_i,
                land_c, land_b, land_a, out_b, out_a, land_m, *sems):
    at = Place(n_mob, n_imm)
    at.barrier()
    mob = reduce_mob_start(at, part_i, land_m, *sems[6:8])
    own_m[...] = conc_m[...] + reduce_imm(at, part_m, land_c, land_b, land_a, out_b, out_a, sems[:6])
    total = conc_i[...] + part_i[at.p]
    for dp, copy in enumerate(mob, 1):
        copy.wait()
        total = total + land_m[dp]
    own_i[...] = total


def split3(x):
    high = x.astype(jnp.bfloat16).astype(jnp.float32)
    rest = x - high
    mid = rest.astype(jnp.bfloat16).astype(jnp.float32)
    return high, mid, rest - mid


def conc_rows(conc):
    high = conc.astype(jnp.bfloat16).astype(jnp.float32)
    ones = jnp.ones_like(conc)
    return jnp.concatenate([high, conc - high, ones, ones], axis=0).astype(jnp.bfloat16)


def pair_loop(step, rows, cols, count, x_pos, x_conc, y_pos, y_conc, gain_m, gain_i, y_split):
    gain_m[...] = jnp.zeros_like(gain_m)
    gain_i[...] = jnp.zeros_like(gain_i)

    def prepare(c, carry):
        h, m, l = split3(y_pos[c])
        zeros = jnp.zeros((128 - 8 * GROUPS, 128), jnp.float32)
        stacked = jnp.concatenate([h, h, h, m, m, l, zeros], axis=0)
        y_split[c] = stacked.T.astype(jnp.bfloat16)
        return carry

    lax.fori_loop(0, y_pos.shape[0], prepare, 0)
    row = lax.broadcasted_iota(jnp.int32, (8, 128), 0)
    keep = row < 4
    unit = jnp.where(row == 4, 1.0, 0.0).astype(jnp.float32)
    zeros = jnp.zeros((128 - 8 * GROUPS, 128), jnp.float32)
    used = count[0, 0]

    def body(block, carry):
        def weigh(u):
            k = block * UNROLL + u
            r, c = rows[0, 0, k], cols[0, 0, k]
            x = x_pos[r]
            if step:
                x = pltpu.roll(x, 4, 0)
            h, m, l = split3(jnp.where(keep, x, unit))
            x_split = jnp.concatenate([h, m, l, h, m, h, zeros], axis=0).astype(jnp.bfloat16)
            power = jnp.dot(y_split[c], x_split, preferred_element_type=jnp.float32)
            return k, r, c, power

        def transfer(k, r, c, power):
            weight = jnp.exp2(power).astype(jnp.bfloat16)
            cm, ci = x_conc[r], y_conc[c]
            to_m = jnp.dot(conc_rows(ci), weight, preferred_element_type=jnp.float32)
            to_i = lax.dot_general(
                conc_rows(cm), weight, (((1,), (1,)), ((), ())), preferred_element_type=jnp.float32
            )
            return k, r, c, cm, ci, to_m, to_i

        def finish(k, r, c, cm, ci, to_m, to_i):
            rate = jnp.where(k < used, RATE, 0.0).astype(jnp.float32)
            add_m = rate * (to_m[0:8] + to_m[8:16] - to_m[16:24] * cm)
            add_i = rate * (to_i[0:8] + to_i[8:16] - to_i[16:24] * ci)
            return r, c, add_m, add_i

        weighed, moved, results = [], [], []
        for u in range(UNROLL + 2):
            if u < UNROLL:
                weighed.append(weigh(u))
            if 1 <= u <= UNROLL:
                moved.append(transfer(*weighed[u - 1]))
            if u >= 2:
                results.append(finish(*moved[u - 2]))
        for r, c, add_m, add_i in results:
            gain_m[r] += add_m
            gain_i[c] += add_i
        return carry

    lax.fori_loop(0, lax.div(used + (UNROLL - 1), UNROLL), body, 0)


def on_device(n_mob, n_imm, mpos, walk, mconc, ipos, iconc, rows, cols, counts):
    rest = n_imm // 2
    nb = 1
    while nb * nb * 4 <= rest:
        nb *= 2
    na = rest // nb
    f32 = jnp.float32
    mc, solutes, part = mconc.shape
    ic = iconc.shape[0]
    vmem = pl.BlockSpec(memory_space=pltpu.VMEM)
    smem = pl.BlockSpec(memory_space=pltpu.SMEM)
    dma = pltpu.SemaphoreType.DMA

    def params(ident):
        return pltpu.CompilerParams(collective_id=ident, has_side_effects=True, vmem_limit_bytes=VMEM_LIMIT)

    def gather_sems(refs):
        return [dma((refs, na))] * 2 + [dma((refs, na, nb))] * 4

    reduce_sems = [dma((na,))] * 2 + [dma((na, nb))] * 4
    cell_m = (mc, solutes, part)
    cell_i = (ic, solutes, part)
    all_m = jax.ShapeDtypeStruct((na, nb, 2) + cell_m, f32)
    all_i = jax.ShapeDtypeStruct((n_mob,) + cell_i, f32)
    g_pos, g_conc, h_pos, h_conc = pl.pallas_call(
        functools.partial(first_gather, n_mob, n_imm),
        out_shape=(all_m, all_m, all_i, all_i),
        in_specs=[vmem] * 5,
        out_specs=(vmem,) * 4,
        scratch_shapes=gather_sems(2) + [dma((2, n_mob))] * 2,
        compiler_params=params(0),
    )(mpos, walk, mconc, ipos, iconc)

    flat_m = (n_imm * mc, solutes, part)
    flat_i = (n_mob * ic, solutes, part)

    def pairs(step, x_conc, y_conc):
        gains = pl.pallas_call(
            functools.partial(pair_loop, step),
            out_shape=(jax.ShapeDtypeStruct(flat_m, f32), jax.ShapeDtypeStruct(flat_i, f32)),
            in_specs=[smem] * 3 + [vmem] * 4,
            out_specs=(vmem,) * 2,
            scratch_shapes=[pltpu.VMEM((flat_i[0], part, 128), jnp.bfloat16)],
            compiler_params=pltpu.CompilerParams(vmem_limit_bytes=VMEM_LIMIT),
        )(
            rows,
            cols,
            counts,
            g_pos.reshape(flat_m),
            x_conc.reshape(flat_m),
            h_pos.reshape(flat_i),
            y_conc.reshape(flat_i),
        )
        return gains[0].reshape(all_m.shape), gains[1].reshape(all_i.shape)

    lands = [
        pltpu.VMEM((na, nb) + cell_m, f32),
        pltpu.VMEM((na, nb) + cell_m, f32),
        pltpu.VMEM((na,) + cell_m, f32),
        pltpu.VMEM((na, nb) + cell_m, f32),
        pltpu.VMEM((na,) + cell_m, f32),
        pltpu.VMEM((n_mob,) + cell_i, f32),
    ]
    own = (jax.ShapeDtypeStruct(cell_m, f32), jax.ShapeDtypeStruct(cell_i, f32))
    part_m, part_i = pairs(0, g_conc, h_conc)
    own_m, own_i, g_conc, h_conc = pl.pallas_call(
        functools.partial(exchange, n_mob, n_imm),
        out_shape=own + (all_m, all_i),
        in_specs=[vmem] * 4,
        out_specs=(vmem,) * 4,
        scratch_shapes=lands + reduce_sems + [dma((n_mob,))] * 2 + [dma((1, n_mob))] * 2 + gather_sems(1),
        compiler_params=params(1),
    )(part_m, part_i, mconc, iconc)
    part_m, part_i = pairs(1, g_conc, h_conc)
    return pl.pallas_call(
        functools.partial(last_reduce, n_mob, n_imm),
        out_shape=own,
        in_specs=[vmem] * 4,
        out_specs=(vmem,) * 2,
        scratch_shapes=lands + reduce_sems + [dma((n_mob,))] * 2,
        compiler_params=params(2),
    )(part_m, part_i, own_m, own_i)


def solution(mesh):
    return jax.shard_map(
        functools.partial(on_device, mesh.shape["mob"], mesh.shape["imm"]),
        mesh=mesh,
        in_specs=(
            P(("mob", "imm"), None, None),
            P(None, ("mob", "imm"), None, None),
            P(("mob", "imm"), None, None),
            P(("mob", "imm"), None, None),
            P(("mob", "imm"), None, None),
            P("mob", "imm", None),
            P("mob", "imm", None),
            P("mob", "imm"),
        ),
        out_specs=(P(("mob", "imm"), None, None), P(("mob", "imm"), None, None)),
        check_vma=False,
    )
```

```python
import functools
import math

import jax
import jax.numpy as jnp
from jax import lax
from jax.experimental import pallas as pl
from jax.experimental.pallas import tpu as pltpu
from jax.sharding import PartitionSpec as P

RATE = 1.0 / 512.0
SCALE = math.sqrt(0.5 * math.log2(math.e))
CENTRE = 2.0
MESH = pl.DeviceIdType.MESH
VMEM_LIMIT = 48 * 1024 * 1024
UNROLL = 64
GROUPS = 6


class Place:
    def __init__(self, n_mob, n_imm):
        rest = n_imm // 2
        nb = 1
        while nb * nb * 4 <= rest:
            nb *= 2
        self.nm, self.nb, self.na = n_mob, nb, rest // nb
        self.p = lax.axis_index("mob")
        q = lax.axis_index("imm")
        self.core = lax.rem(q, 2)
        chip = lax.div(q, 2)
        self.b = lax.rem(chip, nb)
        self.a = lax.div(chip, nb)

    def am(self, d):
        return lax.rem(self.a + (d + self.na), self.na)

    def bm(self, d):
        return lax.rem(self.b + (d + self.nb), self.nb)

    def pm(self, d):
        return lax.rem(self.p + (d + self.nm), self.nm)

    def dev(self, a, b, core):
        return (self.p, (a * self.nb + b) * 2 + core)

    def sibling(self):
        return self.dev(self.a, self.b, 1 - self.core)

    def across(self, d):
        return (self.pm(d), (self.a * self.nb + self.b) * 2 + self.core)

    def barrier(self):
        sem = pltpu.get_barrier_semaphore()
        peers = [self.sibling()]
        peers += [self.dev(self.a, self.bm(d), self.core) for d in range(1, self.nb)]
        peers += [self.dev(self.am(d), self.b, self.core) for d in range(1, self.na)]
        peers += [self.across(d) for d in range(1, self.nm)]
        for peer in peers:
            pl.semaphore_signal(sem, inc=1, device_id=peer, device_id_type=MESH)
        pl.semaphore_wait(sem, len(peers))


def remote(src, dst, send, recv, device):
    copy = pltpu.make_async_remote_copy(
        src_ref=src, dst_ref=dst, send_sem=send, recv_sem=recv, device_id=device, device_id_type=MESH
    )
    copy.start()
    return copy


def gather_imm(at, refs, sems):
    a_send, a_recv, b_send, b_recv, c_send, c_recv = sems
    na, nb = at.na, at.nb
    sends, a_copies, b_copies, c_copies = [], {}, {}, {}
    for da in range(1, na):
        for i, g in enumerate(refs):
            block = g.at[at.a, at.b, at.core]
            a_copies[da, i] = remote(
                block, block, a_send.at[i, da], a_recv.at[i, da], at.dev(at.am(da), at.b, at.core)
            )
    for da in range(na):
        for i, g in enumerate(refs):
            if da:
                a_copies[da, i].wait_recv()
            block = g.at[at.am(-da), at.b, at.core]
            for db in range(1, nb):
                b_copies[da, db, i] = remote(
                    block, block, b_send.at[i, da, db], b_recv.at[i, da, db], at.dev(at.a, at.bm(db), at.core)
                )
            c_copies[da, 0, i] = remote(
                block, block, c_send.at[i, da, 0], c_recv.at[i, da, 0], at.sibling()
            )
    for da in range(na):
        for db in range(1, nb):
            for i, g in enumerate(refs):
                b_copies[da, db, i].wait_recv()
                block = g.at[at.am(-da), at.bm(-db), at.core]
                c_copies[da, db, i] = remote(
                    block, block, c_send.at[i, da, db], c_recv.at[i, da, db], at.sibling()
                )
    for copy in c_copies.values():
        copy.wait_recv()
    for copies in (a_copies, b_copies, c_copies):
        for copy in copies.values():
            copy.wait_send()


def gather_mob_start(at, refs, send, recv):
    copies = []
    for dp in range(1, at.nm):
        for i, g in enumerate(refs):
            block = g.at[at.p]
            copies.append(remote(block, block, send.at[i, dp], recv.at[i, dp], at.across(dp)))
    return copies


def reduce_mob_start(at, part, land, send, recv):
    return [
        remote(part.at[at.pm(dp)], land.at[dp], send.at[dp], recv.at[dp], at.across(dp))
        for dp in range(1, at.nm)
    ]


def reduce_imm(at, part, land_c, land_b, land_a, out_b, out_a, sems):
    a_send, a_recv, b_send, b_recv, c_send, c_recv = sems
    na, nb = at.na, at.nb
    order = list(range(1, na)) + [0]
    a_copies, b_copies, c_copies = {}, {}, {}
    for db in list(range(1, nb)) + [0]:
        for da in order:
            c_copies[da, db] = remote(
                part.at[at.am(da), at.bm(db), 1 - at.core],
                land_c.at[da, db],
                c_send.at[da, db],
                c_recv.at[da, db],
                at.sibling(),
            )
    for da in order:
        for db in range(1, nb):
            c_copies[da, db].wait_recv()
            out_b[da, db] = part[at.am(da), at.bm(db), at.core] + land_c[da, db]
            b_copies[da, db] = remote(
                out_b.at[da, db],
                land_b.at[da, db],
                b_send.at[da, db],
                b_recv.at[da, db],
                at.dev(at.a, at.bm(db), at.core),
            )
    total = None
    for da in order:
        c_copies[da, 0].wait_recv()
        here = part[at.am(da), at.b, at.core] + land_c[da, 0]
        for db in range(1, nb):
            b_copies[da, db].wait_recv()
            here = here + land_b[da, db]
        if da:
            out_a[da] = here
            a_copies[da] = remote(
                out_a.at[da], land_a.at[da], a_send.at[da], a_recv.at[da], at.dev(at.am(da), at.b, at.core)
            )
        else:
            total = here
    for da in range(1, na):
        a_copies[da].wait_recv()
        total = total + land_a[da]
    for copies in (a_copies, b_copies, c_copies):
        for copy in copies.values():
            copy.wait_send()
    return total


def first_gather(n_mob, n_imm, mpos, walk, mconc, ipos, iconc, g_pos, g_conc, h_pos, h_conc, *sems):
    at = Place(n_mob, n_imm)
    own = g_pos.at[at.a, at.b, at.core]
    moved = mpos[...]
    for step in range(2):
        moved = moved + walk[step]
        x = (moved - CENTRE) * SCALE
        own[:, 4 * step : 4 * step + 3, :] = x
        own[:, 4 * step + 3 : 4 * step + 4, :] = -jnp.sum(x * x, axis=1, keepdims=True)
    g_conc[at.a, at.b, at.core] = mconc[...]
    h_own = h_pos.at[at.p]
    y = (ipos[...] - CENTRE) * SCALE
    h_own[:, 0:3, :] = 2.0 * y
    h_own[:, 3:4, :] = jnp.ones_like(y[:, 0:1, :])
    h_own[:, 4:5, :] = -jnp.sum(y * y, axis=1, keepdims=True)
    h_own[:, 5:8, :] = jnp.zeros_like(y)
    h_conc[at.p] = iconc[...]
    at.barrier()
    mob = gather_mob_start(at, (h_pos, h_conc), *sems[6:])
    gather_imm(at, (g_conc, g_pos), sems[:6])
    for copy in mob:
        copy.wait()


def exchange(n_mob, n_imm, part_m, part_i, conc_m, conc_i, own_m, own_i, g_conc, h_conc,
             land_c, land_b, land_a, out_b, out_a, land_m, *sems):
    at = Place(n_mob, n_imm)
    at.barrier()
    mob = reduce_mob_start(at, part_i, land_m, *sems[6:8])
    total = conc_m[...] + reduce_imm(at, part_m, land_c, land_b, land_a, out_b, out_a, sems[:6])
    own_m[...] = total
    g_conc[at.a, at.b, at.core] = total
    total = conc_i[...] + part_i[at.p]
    for dp, copy in enumerate(mob, 1):
        copy.wait()
        total = total + land_m[dp]
    own_i[...] = total
    h_conc[at.p] = total
    mob = gather_mob_start(at, (h_conc,), *sems[8:10])
    gather_imm(at, (g_conc,), sems[10:16])
    for copy in mob:
        copy.wait()


def last_reduce(n_mob, n_imm, part_m, part_i, conc_m, conc_i, own_m, own_i,
                land_c, land_b, land_a, out_b, out_a, land_m, *sems):
    at = Place(n_mob, n_imm)
    at.barrier()
    mob = reduce_mob_start(at, part_i, land_m, *sems[6:8])
    own_m[...] = conc_m[...] + reduce_imm(at, part_m, land_c, land_b, land_a, out_b, out_a, sems[:6])
    total = conc_i[...] + part_i[at.p]
    for dp, copy in enumerate(mob, 1):
        copy.wait()
        total = total + land_m[dp]
    own_i[...] = total


def split3(x):
    high = x.astype(jnp.bfloat16).astype(jnp.float32)
    rest = x - high
    mid = rest.astype(jnp.bfloat16).astype(jnp.float32)
    return high, mid, rest - mid


def conc_rows(conc):
    high = conc.astype(jnp.bfloat16).astype(jnp.float32)
    ones = jnp.ones_like(conc)
    return jnp.concatenate([high, conc - high, ones, ones], axis=0).astype(jnp.bfloat16)


def pair_loop(step, rows, cols, count, x_pos, x_conc, y_pos, y_conc, gain_m, gain_i, y_split):
    gain_m[...] = jnp.zeros_like(gain_m)
    gain_i[...] = jnp.zeros_like(gain_i)

    def prepare(c, carry):
        h, m, l = split3(y_pos[c])
        zeros = jnp.zeros((128 - 8 * GROUPS, 128), jnp.float32)
        stacked = jnp.concatenate([h, h, h, m, m, l, zeros], axis=0)
        y_split[c] = stacked.T.astype(jnp.bfloat16)
        return carry

    lax.fori_loop(0, y_pos.shape[0], prepare, 0)
    row = lax.broadcasted_iota(jnp.int32, (8, 128), 0)
    keep = row < 4
    unit = jnp.where(row == 4, 1.0, 0.0).astype(jnp.float32)
    zeros = jnp.zeros((128 - 8 * GROUPS, 128), jnp.float32)
    used = count[0, 0]

    def body(block, carry):
        def weigh(u):
            k = block * UNROLL + u
            r, c = rows[0, 0, k], cols[0, 0, k]
            x = x_pos[r]
            if step:
                x = pltpu.roll(x, 4, 0)
            h, m, l = split3(jnp.where(keep, x, unit))
            x_split = jnp.concatenate([h, m, l, h, m, h, zeros], axis=0).astype(jnp.bfloat16)
            power = jnp.dot(y_split[c], x_split, preferred_element_type=jnp.float32)
            return k, r, c, power

        def transfer(k, r, c, power):
            weight = jnp.exp2(power).astype(jnp.bfloat16)
            cm, ci = x_conc[r], y_conc[c]
            to_m = jnp.dot(conc_rows(ci), weight, preferred_element_type=jnp.float32)
            to_i = lax.dot_general(
                conc_rows(cm), weight, (((1,), (1,)), ((), ())), preferred_element_type=jnp.float32
            )
            return k, r, c, cm, ci, to_m, to_i

        def finish(k, r, c, cm, ci, to_m, to_i):
            rate = jnp.where(k < used, RATE, 0.0).astype(jnp.float32)
            add_m = rate * (to_m[0:8] + to_m[8:16] - to_m[16:24] * cm)
            add_i = rate * (to_i[0:8] + to_i[8:16] - to_i[16:24] * ci)
            return r, c, add_m, add_i

        weighed, moved, results = [], [], []
        for u in range(UNROLL + 9):
            if u < UNROLL:
                weighed.append(weigh(u))
            if 5 <= u < UNROLL + 5:
                moved.append(transfer(*weighed[u - 5]))
            if u >= 9:
                results.append(finish(*moved[u - 9]))
        for r, c, add_m, add_i in results:
            gain_m[r] += add_m
            gain_i[c] += add_i
        return carry

    lax.fori_loop(0, lax.div(used + (UNROLL - 1), UNROLL), body, 0)


def on_device(n_mob, n_imm, mpos, walk, mconc, ipos, iconc, rows, cols, counts):
    rest = n_imm // 2
    nb = 1
    while nb * nb * 4 <= rest:
        nb *= 2
    na = rest // nb
    f32 = jnp.float32
    mc, solutes, part = mconc.shape
    ic = iconc.shape[0]
    vmem = pl.BlockSpec(memory_space=pltpu.VMEM)
    smem = pl.BlockSpec(memory_space=pltpu.SMEM)
    dma = pltpu.SemaphoreType.DMA

    def params(ident):
        return pltpu.CompilerParams(collective_id=ident, has_side_effects=True, vmem_limit_bytes=VMEM_LIMIT)

    def gather_sems(refs):
        return [dma((refs, na))] * 2 + [dma((refs, na, nb))] * 4

    reduce_sems = [dma((na,))] * 2 + [dma((na, nb))] * 4
    cell_m = (mc, solutes, part)
    cell_i = (ic, solutes, part)
    all_m = jax.ShapeDtypeStruct((na, nb, 2) + cell_m, f32)
    all_i = jax.ShapeDtypeStruct((n_mob,) + cell_i, f32)
    g_pos, g_conc, h_pos, h_conc = pl.pallas_call(
        functools.partial(first_gather, n_mob, n_imm),
        out_shape=(all_m, all_m, all_i, all_i),
        in_specs=[vmem] * 5,
        out_specs=(vmem,) * 4,
        scratch_shapes=gather_sems(2) + [dma((2, n_mob))] * 2,
        compiler_params=params(0),
    )(mpos, walk, mconc, ipos, iconc)

    flat_m = (n_imm * mc, solutes, part)
    flat_i = (n_mob * ic, solutes, part)

    def pairs(step, x_conc, y_conc):
        gains = pl.pallas_call(
            functools.partial(pair_loop, step),
            out_shape=(jax.ShapeDtypeStruct(flat_m, f32), jax.ShapeDtypeStruct(flat_i, f32)),
            in_specs=[smem] * 3 + [vmem] * 4,
            out_specs=(vmem,) * 2,
            scratch_shapes=[pltpu.VMEM((flat_i[0], part, 128), jnp.bfloat16)],
            compiler_params=pltpu.CompilerParams(vmem_limit_bytes=VMEM_LIMIT),
        )(
            rows,
            cols,
            counts,
            g_pos.reshape(flat_m),
            x_conc.reshape(flat_m),
            h_pos.reshape(flat_i),
            y_conc.reshape(flat_i),
        )
        return gains[0].reshape(all_m.shape), gains[1].reshape(all_i.shape)

    lands = [
        pltpu.VMEM((na, nb) + cell_m, f32),
        pltpu.VMEM((na, nb) + cell_m, f32),
        pltpu.VMEM((na,) + cell_m, f32),
        pltpu.VMEM((na, nb) + cell_m, f32),
        pltpu.VMEM((na,) + cell_m, f32),
        pltpu.VMEM((n_mob,) + cell_i, f32),
    ]
    own = (jax.ShapeDtypeStruct(cell_m, f32), jax.ShapeDtypeStruct(cell_i, f32))
    part_m, part_i = pairs(0, g_conc, h_conc)
    own_m, own_i, g_conc, h_conc = pl.pallas_call(
        functools.partial(exchange, n_mob, n_imm),
        out_shape=own + (all_m, all_i),
        in_specs=[vmem] * 4,
        out_specs=(vmem,) * 4,
        scratch_shapes=lands + reduce_sems + [dma((n_mob,))] * 2 + [dma((1, n_mob))] * 2 + gather_sems(1),
        compiler_params=params(1),
    )(part_m, part_i, mconc, iconc)
    part_m, part_i = pairs(1, g_conc, h_conc)
    return pl.pallas_call(
        functools.partial(last_reduce, n_mob, n_imm),
        out_shape=own,
        in_specs=[vmem] * 4,
        out_specs=(vmem,) * 2,
        scratch_shapes=lands + reduce_sems + [dma((n_mob,))] * 2,
        compiler_params=params(2),
    )(part_m, part_i, own_m, own_i)


def solution(mesh):
    return jax.shard_map(
        functools.partial(on_device, mesh.shape["mob"], mesh.shape["imm"]),
        mesh=mesh,
        in_specs=(
            P(("mob", "imm"), None, None),
            P(None, ("mob", "imm"), None, None),
            P(("mob", "imm"), None, None),
            P(("mob", "imm"), None, None),
            P(("mob", "imm"), None, None),
            P("mob", "imm", None),
            P("mob", "imm", None),
            P("mob", "imm"),
        ),
        out_specs=(P(("mob", "imm"), None, None), P(("mob", "imm"), None, None)),
        check_vma=False,
    )
```

```python
import functools
import math

import jax
import jax.numpy as jnp
from jax import lax
from jax.experimental import pallas as pl
from jax.experimental.pallas import tpu as pltpu
from jax.sharding import PartitionSpec as P

RATE = 1.0 / 512.0
SCALE = math.sqrt(0.5 * math.log2(math.e))
CENTRE = 2.0
MESH = pl.DeviceIdType.MESH
VMEM_LIMIT = 48 * 1024 * 1024
UNROLL = 64
GROUPS = 6


class Place:
    def __init__(self, n_mob, n_imm):
        rest = n_imm // 2
        nb = 1
        while nb * nb * 4 <= rest:
            nb *= 2
        self.nm, self.nb, self.na = n_mob, nb, rest // nb
        self.p = lax.axis_index("mob")
        q = lax.axis_index("imm")
        self.core = lax.rem(q, 2)
        chip = lax.div(q, 2)
        self.b = lax.rem(chip, nb)
        self.a = lax.div(chip, nb)

    def am(self, d):
        return lax.rem(self.a + (d + self.na), self.na)

    def bm(self, d):
        return lax.rem(self.b + (d + self.nb), self.nb)

    def pm(self, d):
        return lax.rem(self.p + (d + self.nm), self.nm)

    def dev(self, a, b, core):
        return (self.p, (a * self.nb + b) * 2 + core)

    def sibling(self):
        return self.dev(self.a, self.b, 1 - self.core)

    def across(self, d):
        return (self.pm(d), (self.a * self.nb + self.b) * 2 + self.core)

    def barrier(self):
        sem = pltpu.get_barrier_semaphore()
        peers = [self.sibling()]
        peers += [self.dev(self.a, self.bm(d), self.core) for d in range(1, self.nb)]
        peers += [self.dev(self.am(d), self.b, self.core) for d in range(1, self.na)]
        peers += [self.across(d) for d in range(1, self.nm)]
        for peer in peers:
            pl.semaphore_signal(sem, inc=1, device_id=peer, device_id_type=MESH)
        pl.semaphore_wait(sem, len(peers))


def remote(src, dst, send, recv, device):
    copy = pltpu.make_async_remote_copy(
        src_ref=src, dst_ref=dst, send_sem=send, recv_sem=recv, device_id=device, device_id_type=MESH
    )
    copy.start()
    return copy


def gather_imm(at, refs, sems):
    a_send, a_recv, b_send, b_recv, c_send, c_recv = sems
    na, nb = at.na, at.nb
    sends, a_copies, b_copies, c_copies = [], {}, {}, {}
    for da in range(1, na):
        for i, g in enumerate(refs):
            block = g.at[at.a, at.b, at.core]
            a_copies[da, i] = remote(
                block, block, a_send.at[i, da], a_recv.at[i, da], at.dev(at.am(da), at.b, at.core)
            )
    for da in range(na):
        for i, g in enumerate(refs):
            if da:
                a_copies[da, i].wait_recv()
            block = g.at[at.am(-da), at.b, at.core]
            for db in range(1, nb):
                b_copies[da, db, i] = remote(
                    block, block, b_send.at[i, da, db], b_recv.at[i, da, db], at.dev(at.a, at.bm(db), at.core)
                )
            c_copies[da, 0, i] = remote(
                block, block, c_send.at[i, da, 0], c_recv.at[i, da, 0], at.sibling()
            )
    for da in range(na):
        for db in range(1, nb):
            for i, g in enumerate(refs):
                b_copies[da, db, i].wait_recv()
                block = g.at[at.am(-da), at.bm(-db), at.core]
                c_copies[da, db, i] = remote(
                    block, block, c_send.at[i, da, db], c_recv.at[i, da, db], at.sibling()
                )
    for copy in c_copies.values():
        copy.wait_recv()
    for copies in (a_copies, b_copies, c_copies):
        for copy in copies.values():
            copy.wait_send()


def gather_mob_start(at, refs, send, recv):
    copies = []
    for dp in range(1, at.nm):
        for i, g in enumerate(refs):
            block = g.at[at.p]
            copies.append(remote(block, block, send.at[i, dp], recv.at[i, dp], at.across(dp)))
    return copies


def reduce_mob_start(at, part, land, send, recv):
    return [
        remote(part.at[at.pm(dp)], land.at[dp], send.at[dp], recv.at[dp], at.across(dp))
        for dp in range(1, at.nm)
    ]


def reduce_imm(at, part, land_c, land_b, land_a, out_b, out_a, sems):
    a_send, a_recv, b_send, b_recv, c_send, c_recv = sems
    na, nb = at.na, at.nb
    order = list(range(1, na)) + [0]
    a_copies, b_copies, c_copies = {}, {}, {}
    for db in list(range(1, nb)) + [0]:
        for da in order:
            c_copies[da, db] = remote(
                part.at[at.am(da), at.bm(db), 1 - at.core],
                land_c.at[da, db],
                c_send.at[da, db],
                c_recv.at[da, db],
                at.sibling(),
            )
    for da in order:
        for db in range(1, nb):
            c_copies[da, db].wait_recv()
            out_b[da, db] = part[at.am(da), at.bm(db), at.core] + land_c[da, db]
            b_copies[da, db] = remote(
                out_b.at[da, db],
                land_b.at[da, db],
                b_send.at[da, db],
                b_recv.at[da, db],
                at.dev(at.a, at.bm(db), at.core),
            )
    total = None
    for da in order:
        c_copies[da, 0].wait_recv()
        here = part[at.am(da), at.b, at.core] + land_c[da, 0]
        for db in range(1, nb):
            b_copies[da, db].wait_recv()
            here = here + land_b[da, db]
        if da:
            out_a[da] = here
            a_copies[da] = remote(
                out_a.at[da], land_a.at[da], a_send.at[da], a_recv.at[da], at.dev(at.am(da), at.b, at.core)
            )
        else:
            total = here
    for da in range(1, na):
        a_copies[da].wait_recv()
        total = total + land_a[da]
    for copies in (a_copies, b_copies, c_copies):
        for copy in copies.values():
            copy.wait_send()
    return total


def first_gather(n_mob, n_imm, mpos, walk, mconc, ipos, iconc, g_pos, g_conc, h_pos, h_conc, *sems):
    at = Place(n_mob, n_imm)
    own = g_pos.at[at.a, at.b, at.core]
    moved = mpos[...]
    for step in range(2):
        moved = moved + walk[step]
        x = (moved - CENTRE) * SCALE
        own[:, 4 * step : 4 * step + 3, :] = x
        own[:, 4 * step + 3 : 4 * step + 4, :] = -jnp.sum(x * x, axis=1, keepdims=True)
    g_conc[at.a, at.b, at.core] = mconc[...]
    h_own = h_pos.at[at.p]
    y = (ipos[...] - CENTRE) * SCALE
    h_own[:, 0:3, :] = 2.0 * y
    h_own[:, 3:4, :] = jnp.ones_like(y[:, 0:1, :])
    h_own[:, 4:5, :] = -jnp.sum(y * y, axis=1, keepdims=True)
    h_own[:, 5:8, :] = jnp.zeros_like(y)
    h_conc[at.p] = iconc[...]
    at.barrier()
    mob = gather_mob_start(at, (h_pos, h_conc), *sems[6:])
    gather_imm(at, (g_conc, g_pos), sems[:6])
    for copy in mob:
        copy.wait()


def exchange(n_mob, n_imm, part_m, part_i, conc_m, conc_i, own_m, own_i, g_conc, h_conc,
             land_c, land_b, land_a, out_b, out_a, land_m, *sems):
    at = Place(n_mob, n_imm)
    at.barrier()
    mob = reduce_mob_start(at, part_i, land_m, *sems[6:8])
    total = conc_m[...] + reduce_imm(at, part_m, land_c, land_b, land_a, out_b, out_a, sems[:6])
    own_m[...] = total
    g_conc[at.a, at.b, at.core] = total
    total = conc_i[...] + part_i[at.p]
    for dp, copy in enumerate(mob, 1):
        copy.wait()
        total = total + land_m[dp]
    own_i[...] = total
    h_conc[at.p] = total
    mob = gather_mob_start(at, (h_conc,), *sems[8:10])
    gather_imm(at, (g_conc,), sems[10:16])
    for copy in mob:
        copy.wait()


def last_reduce(n_mob, n_imm, part_m, part_i, conc_m, conc_i, own_m, own_i,
                land_c, land_b, land_a, out_b, out_a, land_m, *sems):
    at = Place(n_mob, n_imm)
    at.barrier()
    mob = reduce_mob_start(at, part_i, land_m, *sems[6:8])
    own_m[...] = conc_m[...] + reduce_imm(at, part_m, land_c, land_b, land_a, out_b, out_a, sems[:6])
    total = conc_i[...] + part_i[at.p]
    for dp, copy in enumerate(mob, 1):
        copy.wait()
        total = total + land_m[dp]
    own_i[...] = total


def split3(x):
    high = x.astype(jnp.bfloat16).astype(jnp.float32)
    rest = x - high
    mid = rest.astype(jnp.bfloat16).astype(jnp.float32)
    return high, mid, rest - mid


def conc_rows(conc):
    high = conc.astype(jnp.bfloat16).astype(jnp.float32)
    ones = jnp.ones_like(conc)
    return jnp.concatenate([high, conc - high, ones, ones], axis=0).astype(jnp.bfloat16)


def pair_loop(step, rows, cols, count, x_pos, x_conc, y_pos, y_conc, gain_m, gain_i, y_split):
    gain_m[...] = jnp.zeros_like(gain_m)
    gain_i[...] = jnp.zeros_like(gain_i)

    def prepare(c, carry):
        h, m, l = split3(y_pos[c])
        zeros = jnp.zeros((128 - 8 * GROUPS, 128), jnp.float32)
        stacked = jnp.concatenate([h, h, h, m, m, l, zeros], axis=0)
        y_split[c] = stacked.T.astype(jnp.bfloat16)
        return carry

    lax.fori_loop(0, y_pos.shape[0], prepare, 0, unroll=8)
    row = lax.broadcasted_iota(jnp.int32, (8, 128), 0)
    keep = row < 4
    unit = jnp.where(row == 4, 1.0, 0.0).astype(jnp.float32)
    zeros = jnp.zeros((128 - 8 * GROUPS, 128), jnp.float32)
    used = count[0, 0]

    def body(block, carry):
        def weigh(u):
            k = block * UNROLL + u
            r, c = rows[0, 0, k], cols[0, 0, k]
            x = x_pos[r]
            if step:
                x = pltpu.roll(x, 4, 0)
            h, m, l = split3(jnp.where(keep, x, unit))
            x_split = jnp.concatenate([h, m, l, h, m, h, zeros], axis=0).astype(jnp.bfloat16)
            power = jnp.dot(y_split[c], x_split, preferred_element_type=jnp.float32)
            return k, r, c, power

        def transfer(k, r, c, power):
            weight = jnp.exp2(power).astype(jnp.bfloat16)
            cm, ci = x_conc[r], y_conc[c]
            to_m = jnp.dot(conc_rows(ci), weight, preferred_element_type=jnp.float32)
            to_i = lax.dot_general(
                conc_rows(cm), weight, (((1,), (1,)), ((), ())), preferred_element_type=jnp.float32
            )
            return k, r, c, cm, ci, to_m, to_i

        def finish(k, r, c, cm, ci, to_m, to_i):
            rate = jnp.where(k < used, RATE, 0.0).astype(jnp.float32)
            add_m = rate * (to_m[0:8] + to_m[8:16] - to_m[16:24] * cm)
            add_i = rate * (to_i[0:8] + to_i[8:16] - to_i[16:24] * ci)
            return r, c, add_m, add_i

        weighed, moved, results = [], [], []
        for u in range(UNROLL + 9):
            if u < UNROLL:
                weighed.append(weigh(u))
            if 5 <= u < UNROLL + 5:
                moved.append(transfer(*weighed[u - 5]))
            if u >= 9:
                results.append(finish(*moved[u - 9]))
        for r, c, add_m, add_i in results:
            gain_m[r] += add_m
            gain_i[c] += add_i
        return carry

    lax.fori_loop(0, lax.div(used + (UNROLL - 1), UNROLL), body, 0)


def on_device(n_mob, n_imm, mpos, walk, mconc, ipos, iconc, rows, cols, counts):
    rest = n_imm // 2
    nb = 1
    while nb * nb * 4 <= rest:
        nb *= 2
    na = rest // nb
    f32 = jnp.float32
    mc, solutes, part = mconc.shape
    ic = iconc.shape[0]
    vmem = pl.BlockSpec(memory_space=pltpu.VMEM)
    smem = pl.BlockSpec(memory_space=pltpu.SMEM)
    dma = pltpu.SemaphoreType.DMA

    def params(ident):
        return pltpu.CompilerParams(collective_id=ident, has_side_effects=True, vmem_limit_bytes=VMEM_LIMIT)

    def gather_sems(refs):
        return [dma((refs, na))] * 2 + [dma((refs, na, nb))] * 4

    reduce_sems = [dma((na,))] * 2 + [dma((na, nb))] * 4
    cell_m = (mc, solutes, part)
    cell_i = (ic, solutes, part)
    all_m = jax.ShapeDtypeStruct((na, nb, 2) + cell_m, f32)
    all_i = jax.ShapeDtypeStruct((n_mob,) + cell_i, f32)
    g_pos, g_conc, h_pos, h_conc = pl.pallas_call(
        functools.partial(first_gather, n_mob, n_imm),
        out_shape=(all_m, all_m, all_i, all_i),
        in_specs=[vmem] * 5,
        out_specs=(vmem,) * 4,
        scratch_shapes=gather_sems(2) + [dma((2, n_mob))] * 2,
        compiler_params=params(0),
    )(mpos, walk, mconc, ipos, iconc)

    flat_m = (n_imm * mc, solutes, part)
    flat_i = (n_mob * ic, solutes, part)

    def pairs(step, x_conc, y_conc):
        gains = pl.pallas_call(
            functools.partial(pair_loop, step),
            out_shape=(jax.ShapeDtypeStruct(flat_m, f32), jax.ShapeDtypeStruct(flat_i, f32)),
            in_specs=[smem] * 3 + [vmem] * 4,
            out_specs=(vmem,) * 2,
            scratch_shapes=[pltpu.VMEM((flat_i[0], part, 128), jnp.bfloat16)],
            compiler_params=pltpu.CompilerParams(vmem_limit_bytes=VMEM_LIMIT),
        )(
            rows,
            cols,
            counts,
            g_pos.reshape(flat_m),
            x_conc.reshape(flat_m),
            h_pos.reshape(flat_i),
            y_conc.reshape(flat_i),
        )
        return gains[0].reshape(all_m.shape), gains[1].reshape(all_i.shape)

    lands = [
        pltpu.VMEM((na, nb) + cell_m, f32),
        pltpu.VMEM((na, nb) + cell_m, f32),
        pltpu.VMEM((na,) + cell_m, f32),
        pltpu.VMEM((na, nb) + cell_m, f32),
        pltpu.VMEM((na,) + cell_m, f32),
        pltpu.VMEM((n_mob,) + cell_i, f32),
    ]
    own = (jax.ShapeDtypeStruct(cell_m, f32), jax.ShapeDtypeStruct(cell_i, f32))
    part_m, part_i = pairs(0, g_conc, h_conc)
    own_m, own_i, g_conc, h_conc = pl.pallas_call(
        functools.partial(exchange, n_mob, n_imm),
        out_shape=own + (all_m, all_i),
        in_specs=[vmem] * 4,
        out_specs=(vmem,) * 4,
        scratch_shapes=lands + reduce_sems + [dma((n_mob,))] * 2 + [dma((1, n_mob))] * 2 + gather_sems(1),
        compiler_params=params(1),
    )(part_m, part_i, mconc, iconc)
    part_m, part_i = pairs(1, g_conc, h_conc)
    return pl.pallas_call(
        functools.partial(last_reduce, n_mob, n_imm),
        out_shape=own,
        in_specs=[vmem] * 4,
        out_specs=(vmem,) * 2,
        scratch_shapes=lands + reduce_sems + [dma((n_mob,))] * 2,
        compiler_params=params(2),
    )(part_m, part_i, own_m, own_i)


def solution(mesh):
    return jax.shard_map(
        functools.partial(on_device, mesh.shape["mob"], mesh.shape["imm"]),
        mesh=mesh,
        in_specs=(
            P(("mob", "imm"), None, None),
            P(None, ("mob", "imm"), None, None),
            P(("mob", "imm"), None, None),
            P(("mob", "imm"), None, None),
            P(("mob", "imm"), None, None),
            P("mob", "imm", None),
            P("mob", "imm", None),
            P("mob", "imm"),
        ),
        out_specs=(P(("mob", "imm"), None, None), P(("mob", "imm"), None, None)),
        check_vma=False,
    )
```
